32 devices in a mesh: pipe: 8 (over z, core), dp: 2 (over y), tensor: 2 (over x).
Axes of the slice: x: 2, y: 2, z: 4, core: 2. Of those that a mesh axis runs over, the one named last changes fastest.
Arguments:
- ssm_output: bfloat16 [8, 2, 1024, 8192], P('pipe', 'dp', None, 'tensor'), may hold values from -6 to 6
- out_weight: bfloat16 [8, 8192, 4096], P('pipe', 'tensor', 'dp'), may hold values from -0.0625 to 0.0625
- in_weight: bfloat16 [8, 4096, 2048], P('pipe', 'dp', 'tensor'), may hold values from -0.09375 to 0.09375
- gain: float32 [8, 4096], P('pipe'), may hold values from 0.1 to 1.9
- residual: bfloat16 [8, 2, 1024, 4096], P('pipe', 'dp', 'tensor'), may hold values from -1.5 to 1.5
- proj_cotangent: bfloat16 [8, 2, 1024, 2048], P('pipe', 'dp', None, 'tensor'), may hold values from -6 to 6
- stream_cotangent: bfloat16 [8, 2, 1024, 4096], P('pipe', 'dp', 'tensor'), may hold values from -12 to 12
Outputs:
- stream: bfloat16 [8, 2, 1024, 4096], P('pipe', 'dp', 'tensor')
- b_proj: bfloat16 [8, 2, 1024, 2048], P('pipe', 'dp', None, 'tensor')
- residual_grad: bfloat16 [8, 2, 1024, 4096], P('pipe', 'dp', 'tensor')
- gain_grad: float32 [8, 4096], P('pipe')
The draws below stay inside these ranges and needn't reach their ends.
All inputs are finite; a program needn't handle non-finite values.
Results may differ from the reference program's by a relative error of at most 0.014.
Values may be sent and summed in bfloat16 or wider, within the bound.
A program may use at most 192 MiB of HBM per device.

```python
import math
import jax
import jax.numpy as jnp
from jax import lax

D = 4096
INNER = 8192
GS = 2048
LAYERS = 118
MB_TOK = 1024
SECTIONS = 8
SEQS = 2
N_TENSOR = 2


def block_levels(key, shape, shards, least, high):
    level, own = 1.0, jax.random.fold_in(key, 6)
    for dim, blocks in shards:
        draws = jnp.exp(jax.random.uniform(jax.random.fold_in(own, dim), (blocks,), jnp.float32, least / len(shards), high / len(shards)))
        level = level * jnp.repeat(draws, shape[dim] // blocks).reshape([-1 if axis == dim else 1 for axis in range(len(shape))])
    return level


def gaussian(rng, shape, width, bound, shards=(), kind=jnp.bfloat16):
    drawn = jax.random.normal(rng, shape, jnp.float32) * width
    if len(shards) > 0:
        drawn = block_levels(rng, shape, shards, -0.22, 0.18) * drawn
    return jnp.clip(drawn, min=-bound, max=bound).astype(kind)


def setup_inputs(seed: int = 0) -> dict:
    streams_of = jax.random.split(jax.random.key(seed), 8)
    return {
        "ssm_output": gaussian(streams_of[0], (SECTIONS, SEQS, MB_TOK, INNER), 1.0, 6.0, ((0, 8), (1, 2), (3, 2))),
        "out_weight": gaussian(streams_of[1], (SECTIONS, INNER, D), INNER ** -0.5, 0.0625, ((0, 8), (1, 2), (2, 2))),
        "in_weight": gaussian(streams_of[2], (SECTIONS, D, GS), D ** -0.5, 0.09375, ((0, 8), (1, 2), (2, 2))),
        "gain": jnp.clip(1.0 + 0.18 * jax.random.normal(streams_of[3], (SECTIONS, D), jnp.float32), 0.1, 1.9),
        "residual": gaussian(streams_of[4], (SECTIONS, SEQS, MB_TOK, D), 0.25, 1.5, ((0, 8), (1, 2), (2, 2))),
        "proj_cotangent": gaussian(streams_of[5], (SECTIONS, SEQS, MB_TOK, GS), 1.0, 6.0, ((0, 8), (1, 2), (3, 2))),
        "stream_cotangent": gaussian(streams_of[6], (SECTIONS, SEQS, MB_TOK, D), 2.0, 12.0, ((0, 8), (1, 2), (2, 2))),
    }


def rounded_sum(partials):
    narrow = lax.optimization_barrier(partials.astype(jnp.bfloat16))
    return lax.optimization_barrier(jnp.sum(narrow.astype(jnp.float32), axis=0))

def reference(ssm_output, out_weight, in_weight, gain, residual, proj_cotangent, stream_cotangent):
    depth_scale = 1.0 / math.sqrt(2.0 * LAYERS)
    width_inner = INNER // N_TENSOR
    width_cols = GS // N_TENSOR

    def mix_section(section_pair):
        ssm_rows, weight_out = section_pair
        blocked = ssm_rows.astype(jnp.float32).reshape(SEQS, MB_TOK, N_TENSOR, width_inner)
        weight_blocks = weight_out.astype(jnp.float32).reshape(N_TENSOR, width_inner, D)
        partials = jnp.einsum('stkc,kcd->kstd', blocked, weight_blocks)
        return rounded_sum(partials)
    mixed_sum = lax.map(mix_section, (ssm_output, out_weight))
    stream = (jnp.roll(residual, 1, 0).astype(jnp.float32) + depth_scale * jnp.roll(mixed_sum, 1, 0)).astype(jnp.bfloat16)

    def section_rest(section_items):
        stream_rows, gain_row, weight_in, cot_proj, cot_stream = section_items
        stream_f32 = stream_rows.astype(jnp.float32)
        inv_rms = lax.rsqrt(lax.optimization_barrier(jnp.mean(stream_f32 * stream_f32, axis=-1, keepdims=True)) + 1e-05)
        unit_rows = stream_f32 * inv_rms
        normed = (unit_rows * gain_row).astype(jnp.bfloat16)
        projected = jnp.einsum('std,dc->stc', normed.astype(jnp.float32), weight_in.astype(jnp.float32)).astype(jnp.bfloat16)
        cot_blocks = cot_proj.astype(jnp.float32).reshape(SEQS, MB_TOK, N_TENSOR, width_cols)
        weight_blocks = weight_in.astype(jnp.float32).reshape(D, N_TENSOR, width_cols)
        partials = jnp.einsum('stkc,dkc->kstd', cot_blocks, weight_blocks)
        normed_grad = rounded_sum(partials)
        gain_part = lax.optimization_barrier(jnp.sum(normed_grad * unit_rows, axis=(0, 1)))
        weighted = gain_row * normed_grad
        centre = lax.optimization_barrier(jnp.mean(weighted * unit_rows, axis=-1, keepdims=True))
        stream_grad = (cot_stream.astype(jnp.float32) + inv_rms * (weighted - unit_rows * centre)).astype(jnp.bfloat16)
        return (projected, stream_grad, gain_part)
    b_proj, stream_grad, gain_grad = lax.map(section_rest, (stream, gain, in_weight, proj_cotangent, stream_cotangent))
    residual_grad = jnp.roll(stream_grad, -1, 0)
    return (stream, b_proj, residual_grad, gain_grad)
```

```python
import functools
import math

import jax
import jax.numpy as jnp
from jax import lax
from jax.sharding import PartitionSpec as P

LAYERS = 118
PARTS = 4


def shifted(block, axis, distance):
    devices = range(lax.axis_size(axis))
    route = [((i - distance) % len(devices), i) for i in devices]
    return lax.ppermute(block, axis, route)


def general_body(ssm_output, out_weight, in_weight, gain, residual, proj_cotangent, stream_cotangent):
    depth_scale = 1.0 / math.sqrt(2.0 * LAYERS)
    out_all, in_all = (
        lax.all_gather(out_weight, "dp", axis=2, tiled=True),
        lax.all_gather(in_weight, "dp", axis=1, tiled=True),
    )
    w_out = out_all[0]
    w_in = in_all[0]
    ssm_rows = ssm_output[0]
    gain_row = gain[0]
    resid_rows = residual[0]
    cot_proj = proj_cotangent[0]
    cot_stream = stream_cotangent[0]
    block = ssm_rows
    mixed_sum = jnp.transpose(
        lax.psum_scatter(
            jnp.einsum("mtc,cd->tmd", block, w_out, preferred_element_type=jnp.float32).astype(
                jnp.bfloat16
            ),
            "tensor",
            scatter_dimension=0,
            tiled=True,
        ).astype(jnp.float32),
        (1, 0, 2),
    )
    own_stream = (resid_rows.astype(jnp.float32) + depth_scale * mixed_sum).astype(jnp.bfloat16)
    stream_rows = shifted(own_stream, "pipe", 1)
    stream_f32 = stream_rows.astype(jnp.float32)
    inv_rms = lax.rsqrt(jnp.mean(stream_f32 * stream_f32, axis=-1, keepdims=True) + 1e-05)
    unit_rows = stream_f32 * inv_rms
    normed = (unit_rows * gain_row).astype(jnp.bfloat16)
    projected = jnp.einsum(
        "mtd,dc->mtc",
        lax.all_gather(normed, "tensor", axis=1, tiled=True),
        w_in,
        preferred_element_type=jnp.float32,
    ).astype(jnp.bfloat16)
    block = cot_proj
    normed_grad = jnp.transpose(
        lax.psum_scatter(
            jnp.einsum("mtc,dc->tmd", block, w_in, preferred_element_type=jnp.float32).astype(
                jnp.bfloat16
            ),
            "tensor",
            scatter_dimension=0,
            tiled=True,
        ).astype(jnp.float32),
        (1, 0, 2),
    )
    gain_part = jnp.sum(normed_grad * unit_rows, axis=(0, 1))
    weighted = gain_row * normed_grad
    centre = jnp.mean(weighted * unit_rows, axis=-1, keepdims=True)
    stream_grad = (
        cot_stream.astype(jnp.float32) + inv_rms * (weighted - unit_rows * centre)
    ).astype(jnp.bfloat16)
    resid_grad = shifted(stream_grad, "pipe", -1)
    stream_rows, projected, resid_grad, gain_part = (stream_rows, projected, resid_grad, gain_part)
    gain_total = lax.psum(gain_part, ("dp", "tensor"))
    return (stream_rows[None], projected[None], resid_grad[None], gain_total[None])


def swapped(block, axis):
    return lax.ppermute(block, axis, [(0, 1), (1, 0)])


def after(block, *earlier):
    return lax.optimization_barrier((block,) + earlier)[0]


def paired_body(parts, ssm_output, out_weight, in_weight, gain, residual, proj_cotangent, stream_cotangent):
    scale = 1.0 / math.sqrt(2.0 * LAYERS)
    j, k = lax.axis_index("dp"), lax.axis_index("tensor")
    rows, cot, v, w = ssm_output[0, 0], proj_cotangent[0, 0], in_weight[0], out_weight[0]
    tokens, half_d = rows.shape[0], w.shape[1]
    half = tokens // 2
    step = half // parts
    gain_row = gain[0]
    resid, cot_stream = residual[0, 0], stream_cotangent[0, 0]
    rows_own = lax.dynamic_slice_in_dim(rows, k * half, half, 0)
    rows_far = lax.dynamic_slice_in_dim(rows, (1 - k) * half, half, 0)
    cot_own = lax.dynamic_slice_in_dim(cot, k * half, half, 0)
    cot_far = lax.dynamic_slice_in_dim(cot, (1 - k) * half, half, 0)
    f32, bf16 = jnp.float32, jnp.bfloat16

    def dot(a, b):
        return jnp.dot(a, b, preferred_element_type=f32)

    def back(a, b):
        return lax.dot_general(a, b, (((1,), (1,)), ((), ())), preferred_element_type=f32).astype(bf16)

    def halves(own, far):
        return jnp.concatenate([jnp.where(j == 0, own, far), jnp.where(j == 0, far, own)], axis=-1)

    v_far = swapped(v, "dp")
    blocks = rows.reshape(2, parts, step, rows.shape[1])
    arrived = []
    for c in range(parts):
        block = after(blocks[:, c], v_far) if c < 2 else after(blocks[:, c], arrived[c - 2])
        arrived.append(swapped(block, "dp"))
    back_own_far = swapped(back(cot_far, v), "tensor")
    mixed_far = swapped(dot(rows_far, w).astype(bf16), "tensor")
    mixed_own = dot(rows_own, w).astype(bf16).astype(f32) + mixed_far.astype(f32)
    grad_own = back(cot_own, v).astype(f32) + back_own_far.astype(f32)
    back_far_far = swapped(back(cot_far, v_far), "tensor")
    grad_far = back(cot_own, v_far).astype(f32) + back_far_far.astype(f32)
    v_all = jnp.concatenate([jnp.where(j == 0, v, v_far), jnp.where(j == 0, v_far, v)], axis=0)
    streams, grads, near, across = [], [], [], []
    gain_part = 0.0
    for c in range(parts):
        take = slice(c * step, (c + 1) * step)
        block = arrived[c]
        to_far = lax.dynamic_index_in_dim(block, 1 - k, 0, keepdims=False)
        to_own = lax.dynamic_index_in_dim(block, k, 0, keepdims=False)
        summed = swapped(dot(to_far, w).astype(bf16), "tensor")
        mixed = (dot(to_own, w).astype(bf16).astype(f32) + summed.astype(f32)).astype(bf16)
        returned = swapped(mixed, "dp").astype(f32)
        own_stream = (resid[take].astype(f32) + scale * halves(mixed_own[take], returned)).astype(bf16)
        stream = shifted(own_stream, "pipe", 1)
        streams.append(stream)
        s = stream.astype(f32)
        inv = lax.rsqrt(jnp.mean(s * s, axis=-1, keepdims=True) + 1e-05)
        unit = s * inv
        normed = (unit * gain_row).astype(bf16)
        normed_far = swapped(normed, "tensor")
        near.append(dot(normed, v_all).astype(bf16))
        across.append(dot(normed_far, v_all).astype(bf16))
        grad = halves(grad_own[take], grad_far[take])
        gain_part = gain_part + jnp.sum(grad * unit, axis=0)
        weighted = gain_row * grad
        centre = jnp.mean(weighted * unit, axis=-1, keepdims=True)
        out = (cot_stream[take].astype(f32) + inv * (weighted - unit * centre)).astype(bf16)
        grads.append(shifted(out, "pipe", -1))
    gain_part = gain_part + swapped(gain_part, "tensor")
    gain_part = gain_part + swapped(gain_part, "dp")
    near, across = jnp.concatenate(near, 0), jnp.concatenate(across, 0)
    projected = jnp.concatenate([jnp.where(k == 0, near, across), jnp.where(k == 0, across, near)], 0)
    return (
        jnp.concatenate(streams, 0)[None, None],
        projected[None, None],
        jnp.concatenate(grads, 0)[None, None],
        gain_part[None],
    )


def solution(mesh):
    in_specs = (
        P("pipe", "dp", None, "tensor"),
        P("pipe", "tensor", "dp"),
        P("pipe", "dp", "tensor"),
        P("pipe", None),
        P("pipe", "dp", "tensor", None),
        P("pipe", "dp", None, "tensor"),
        P("pipe", "dp", "tensor", None),
    )
    out_specs = (
        P("pipe", "dp", "tensor", None),
        P("pipe", "dp", None, "tensor"),
        P("pipe", "dp", "tensor", None),
        P("pipe", None),
    )
    paired = mesh.shape["dp"] == 2 and mesh.shape["tensor"] == 2
    body = functools.partial(paired_body, PARTS) if paired else general_body
    return jax.shard_map(body, mesh=mesh, in_specs=in_specs, out_specs=out_specs, check_vma=False)
```

```python
import functools
import math

import jax
import jax.numpy as jnp
from jax import lax
from jax.sharding import PartitionSpec as P

LAYERS = 118
SHARES = (2, 2, 2, 1, 1)


def shifted(block, axis, distance):
    devices = range(lax.axis_size(axis))
    route = [((i - distance) % len(devices), i) for i in devices]
    return lax.ppermute(block, axis, route)


def general_body(ssm_output, out_weight, in_weight, gain, residual, proj_cotangent, stream_cotangent):
    depth_scale = 1.0 / math.sqrt(2.0 * LAYERS)
    out_all, in_all = (
        lax.all_gather(out_weight, "dp", axis=2, tiled=True),
        lax.all_gather(in_weight, "dp", axis=1, tiled=True),
    )
    w_out = out_all[0]
    w_in = in_all[0]
    ssm_rows = ssm_output[0]
    gain_row = gain[0]
    resid_rows = residual[0]
    cot_proj = proj_cotangent[0]
    cot_stream = stream_cotangent[0]
    block = ssm_rows
    mixed_sum = jnp.transpose(
        lax.psum_scatter(
            jnp.einsum("mtc,cd->tmd", block, w_out, preferred_element_type=jnp.float32).astype(
                jnp.bfloat16
            ),
            "tensor",
            scatter_dimension=0,
            tiled=True,
        ).astype(jnp.float32),
        (1, 0, 2),
    )
    own_stream = (resid_rows.astype(jnp.float32) + depth_scale * mixed_sum).astype(jnp.bfloat16)
    stream_rows = shifted(own_stream, "pipe", 1)
    stream_f32 = stream_rows.astype(jnp.float32)
    inv_rms = lax.rsqrt(jnp.mean(stream_f32 * stream_f32, axis=-1, keepdims=True) + 1e-05)
    unit_rows = stream_f32 * inv_rms
    normed = (unit_rows * gain_row).astype(jnp.bfloat16)
    projected = jnp.einsum(
        "mtd,dc->mtc",
        lax.all_gather(normed, "tensor", axis=1, tiled=True),
        w_in,
        preferred_element_type=jnp.float32,
    ).astype(jnp.bfloat16)
    block = cot_proj
    normed_grad = jnp.transpose(
        lax.psum_scatter(
            jnp.einsum("mtc,dc->tmd", block, w_in, preferred_element_type=jnp.float32).astype(
                jnp.bfloat16
            ),
            "tensor",
            scatter_dimension=0,
            tiled=True,
        ).astype(jnp.float32),
        (1, 0, 2),
    )
    gain_part = jnp.sum(normed_grad * unit_rows, axis=(0, 1))
    weighted = gain_row * normed_grad
    centre = jnp.mean(weighted * unit_rows, axis=-1, keepdims=True)
    stream_grad = (
        cot_stream.astype(jnp.float32) + inv_rms * (weighted - unit_rows * centre)
    ).astype(jnp.bfloat16)
    resid_grad = shifted(stream_grad, "pipe", -1)
    stream_rows, projected, resid_grad, gain_part = (stream_rows, projected, resid_grad, gain_part)
    gain_total = lax.psum(gain_part, ("dp", "tensor"))
    return (stream_rows[None], projected[None], resid_grad[None], gain_total[None])


def swapped(block, axis):
    return lax.ppermute(block, axis, [(0, 1), (1, 0)])


class Order:
    def __init__(self):
        self.last = None

    def step(self, fn, *args):
        if self.last is not None:
            args = lax.optimization_barrier(args + (self.last,))[:-1]
        out = fn(*args)
        self.last = out[0] if isinstance(out, tuple) else out
        return out


def paired_body(shares, ssm_output, out_weight, in_weight, gain, residual, proj_cotangent, stream_cotangent):
    scale = 1.0 / math.sqrt(2.0 * LAYERS)
    j, k = lax.axis_index("dp"), lax.axis_index("tensor")
    rows, cot, v, w = ssm_output[0, 0], proj_cotangent[0, 0], in_weight[0], out_weight[0]
    tokens = rows.shape[0]
    half = tokens // 2
    unit_rows = half // sum(shares)
    bounds = [unit_rows * sum(shares[:i]) for i in range(len(shares) + 1)]
    takes = [slice(a, b) for a, b in zip(bounds, bounds[1:])]
    gain_row = gain[0]
    resid, cot_stream = residual[0, 0], stream_cotangent[0, 0]
    f32, bf16 = jnp.float32, jnp.bfloat16

    def mine(x):
        return lax.dynamic_slice_in_dim(x, k * half, half, 0)

    def others(x):
        return lax.dynamic_slice_in_dim(x, (1 - k) * half, half, 0)

    def dot(a, b):
        return jnp.dot(a, b, preferred_element_type=f32).astype(bf16)

    def back(a, b):
        return lax.dot_general(a, b, (((1,), (1,)), ((), ())), preferred_element_type=f32).astype(bf16)

    def halves(own, far):
        return jnp.concatenate([jnp.where(j == 0, own, far), jnp.where(j == 0, far, own)], axis=-1)

    def add(a, b):
        return a.astype(f32) + b.astype(f32)

    order = Order()
    count = len(takes)
    paired = rows.reshape(2, half, rows.shape[1])
    v_far = swapped(v, "dp")
    arrived, got = [], {}

    def send(c):
        block = paired[:, takes[c]]
        gate = None if c == 0 else v_far if c == 1 else arrived[c - 2]
        if gate is not None:
            block = lax.optimization_barrier((block, gate))[0]
        arrived.append(swapped(block, "dp"))

    send(0)
    back_near = swapped(order.step(lambda a, b: back(others(a), b), cot, v), "tensor")
    mixed_near = swapped(order.step(lambda a, b: dot(others(a), b), rows, w), "tensor")
    mixed_own = order.step(lambda a, b: dot(mine(a), b), rows, w)
    back_own = order.step(lambda a, b: back(mine(a), b), cot, v)
    back_away = swapped(order.step(lambda a, b: back(others(a), b), cot, v_far), "tensor")
    send(1)
    back_far = order.step(lambda a, b: back(mine(a), b), cot, v_far)
    v_all = order.step(
        lambda a, b: jnp.concatenate([jnp.where(j == 0, a, b), jnp.where(j == 0, b, a)], axis=0), v, v_far
    )
    summed, kept, returned, stream, normed, grads, near, across = {}, {}, {}, {}, {}, {}, {}, {}
    gain_part = None

    def multiply(c):
        half_of = lambda x, i: lax.dynamic_index_in_dim(x, i, 0, keepdims=False)
        summed[c] = swapped(order.step(lambda x: dot(half_of(x, 1 - k), w), arrived[c]), "tensor")
        if c + 2 < count:
            send(c + 2)
        kept[c] = order.step(lambda x: dot(half_of(x, k), w), arrived[c])

    def give_back(c):
        returned[c] = swapped(order.step(lambda a, b: add(a, b).astype(bf16), kept[c], summed[c]), "dp")

    def finish_stream(c):
        t = takes[c]

        def fn(back_half, own, far, res):
            total = halves(add(own[t], far[t]), back_half.astype(f32))
            return (res[t].astype(f32) + scale * total).astype(bf16)

        stream[c] = shifted(order.step(fn, returned[c], mixed_own, mixed_near, resid), "pipe", 1)

    def normalise(c):
        nonlocal gain_part
        t = takes[c]

        def norm(s):
            s = s.astype(f32)
            inv = lax.rsqrt(jnp.mean(s * s, axis=-1, keepdims=True) + 1e-05)
            return ((s * inv) * gain_row).astype(bf16), inv

        normed[c], inv = order.step(norm, stream[c])
        got[c] = swapped(normed[c], "tensor")

        def finish(s, inv, own, own_in, far, far_in, cots):
            unit = s.astype(f32) * inv
            grad = halves(add(own[t], own_in[t]), add(far[t], far_in[t]))
            gains = jnp.sum(grad * unit, axis=0)
            weighted = gain_row * grad
            centre = jnp.mean(weighted * unit, axis=-1, keepdims=True)
            return (cots[t].astype(f32) + inv * (weighted - unit * centre)).astype(bf16), gains

        out, gains = order.step(
            finish, stream[c], inv, back_own, back_near, back_far, back_away, cot_stream
        )
        gain_part = gains if gain_part is None else gain_part + gains
        grads[c] = shifted(out, "pipe", -1)

    def project(c):
        near[c] = order.step(dot, normed[c], v_all)
        across[c] = order.step(dot, got[c], v_all)

    for i in range(count + 2):
        if i < count:
            multiply(i)
        if 1 <= i <= count:
            finish_stream(i - 1)
        if 2 <= i:
            project(i - 2)
        if i < count:
            give_back(i)
        if 1 <= i <= count:
            normalise(i - 1)
            if i == count:
                gain_part = gain_part + swapped(gain_part, "tensor")
                gain_part = gain_part + swapped(gain_part, "dp")

    def joined(parts):
        return jnp.concatenate([parts[c] for c in range(count)], 0)

    low, high = joined(near), joined(across)
    projected = jnp.concatenate([jnp.where(k == 0, low, high), jnp.where(k == 0, high, low)], 0)
    return joined(stream)[None, None], projected[None, None], joined(grads)[None, None], gain_part[None]


def solution(mesh):
    in_specs = (
        P("pipe", "dp", None, "tensor"),
        P("pipe", "tensor", "dp"),
        P("pipe", "dp", "tensor"),
        P("pipe", None),
        P("pipe", "dp", "tensor", None),
        P("pipe", "dp", None, "tensor"),
        P("pipe", "dp", "tensor", None),
    )
    out_specs = (
        P("pipe", "dp", "tensor", None),
        P("pipe", "dp", None, "tensor"),
        P("pipe", "dp", "tensor", None),
        P("pipe", None),
    )
    paired = mesh.shape["dp"] == 2 and mesh.shape["tensor"] == 2
    body = functools.partial(paired_body, SHARES) if paired else general_body
    return jax.shard_map(body, mesh=mesh, in_specs=in_specs, out_specs=out_specs, check_vma=False)
```

```python
import functools
import math

import jax
import jax.numpy as jnp
from jax import lax
from jax.sharding import PartitionSpec as P

LAYERS = 118
SHARES = (2, 2, 2, 1, 1)


def shifted(block, axis, distance):
    devices = range(lax.axis_size(axis))
    route = [((i - distance) % len(devices), i) for i in devices]
    return lax.ppermute(block, axis, route)


def general_body(ssm_output, out_weight, in_weight, gain, residual, proj_cotangent, stream_cotangent):
    depth_scale = 1.0 / math.sqrt(2.0 * LAYERS)
    out_all, in_all = (
        lax.all_gather(out_weight, "dp", axis=2, tiled=True),
        lax.all_gather(in_weight, "dp", axis=1, tiled=True),
    )
    w_out = out_all[0]
    w_in = in_all[0]
    ssm_rows = ssm_output[0]
    gain_row = gain[0]
    resid_rows = residual[0]
    cot_proj = proj_cotangent[0]
    cot_stream = stream_cotangent[0]
    block = ssm_rows
    mixed_sum = jnp.transpose(
        lax.psum_scatter(
            jnp.einsum("mtc,cd->tmd", block, w_out, preferred_element_type=jnp.float32).astype(
                jnp.bfloat16
            ),
            "tensor",
            scatter_dimension=0,
            tiled=True,
        ).astype(jnp.float32),
        (1, 0, 2),
    )
    own_stream = (resid_rows.astype(jnp.float32) + depth_scale * mixed_sum).astype(jnp.bfloat16)
    stream_rows = shifted(own_stream, "pipe", 1)
    stream_f32 = stream_rows.astype(jnp.float32)
    inv_rms = lax.rsqrt(jnp.mean(stream_f32 * stream_f32, axis=-1, keepdims=True) + 1e-05)
    unit_rows = stream_f32 * inv_rms
    normed = (unit_rows * gain_row).astype(jnp.bfloat16)
    projected = jnp.einsum(
        "mtd,dc->mtc",
        lax.all_gather(normed, "tensor", axis=1, tiled=True),
        w_in,
        preferred_element_type=jnp.float32,
    ).astype(jnp.bfloat16)
    block = cot_proj
    normed_grad = jnp.transpose(
        lax.psum_scatter(
            jnp.einsum("mtc,dc->tmd", block, w_in, preferred_element_type=jnp.float32).astype(
                jnp.bfloat16
            ),
            "tensor",
            scatter_dimension=0,
            tiled=True,
        ).astype(jnp.float32),
        (1, 0, 2),
    )
    gain_part = jnp.sum(normed_grad * unit_rows, axis=(0, 1))
    weighted = gain_row * normed_grad
    centre = jnp.mean(weighted * unit_rows, axis=-1, keepdims=True)
    stream_grad = (
        cot_stream.astype(jnp.float32) + inv_rms * (weighted - unit_rows * centre)
    ).astype(jnp.bfloat16)
    resid_grad = shifted(stream_grad, "pipe", -1)
    stream_rows, projected, resid_grad, gain_part = (stream_rows, projected, resid_grad, gain_part)
    gain_total = lax.psum(gain_part, ("dp", "tensor"))
    return (stream_rows[None], projected[None], resid_grad[None], gain_total[None])


def swapped(block, axis):
    return lax.ppermute(block, axis, [(0, 1), (1, 0)])


class Order:
    def __init__(self):
        self.last = None

    def step(self, fn, *args):
        if self.last is not None:
            args = lax.optimization_barrier(args + (self.last,))[:-1]
        out = fn(*args)
        self.last = out[0] if isinstance(out, tuple) else out
        return out


def paired_body(shares, ssm_output, out_weight, in_weight, gain, residual, proj_cotangent, stream_cotangent):
    scale = 1.0 / math.sqrt(2.0 * LAYERS)
    j, k = lax.axis_index("dp"), lax.axis_index("tensor")
    rows, cot, v, w = ssm_output[0, 0], proj_cotangent[0, 0], in_weight[0], out_weight[0]
    tokens = rows.shape[0]
    half = tokens // 2
    unit_rows = half // sum(shares)
    bounds = [unit_rows * sum(shares[:i]) for i in range(len(shares) + 1)]
    takes = [slice(a, b) for a, b in zip(bounds, bounds[1:])]
    gain_row = gain[0]
    resid, cot_stream = residual[0, 0], stream_cotangent[0, 0]
    f32, bf16 = jnp.float32, jnp.bfloat16

    def mine(x):
        return lax.dynamic_slice_in_dim(x, k * half, half, 0)

    def others(x):
        return lax.dynamic_slice_in_dim(x, (1 - k) * half, half, 0)

    def dot(a, b):
        return jnp.dot(a, b, preferred_element_type=f32).astype(bf16)

    def back(a, b):
        return lax.dot_general(a, b, (((1,), (1,)), ((), ())), preferred_element_type=f32).astype(bf16)

    def halves(own, far):
        return jnp.concatenate([jnp.where(j == 0, own, far), jnp.where(j == 0, far, own)], axis=-1)

    def add(a, b):
        return a.astype(f32) + b.astype(f32)

    order = Order()
    count = len(takes)
    paired = rows.reshape(2, half, rows.shape[1])
    v_far = swapped(v, "dp")
    arrived, got = [], {}

    def send(c):
        block = paired[:, takes[c]]
        if c > 0:
            block = lax.optimization_barrier((block, gates[c - 1]))[0]
        arrived.append(swapped(block, "dp"))

    send(0)
    back_near = swapped(order.step(lambda a, b: back(others(a), b), cot, v), "tensor")
    mixed_near = swapped(order.step(lambda a, b: dot(others(a), b), rows, w), "tensor")
    mixed_own = order.step(lambda a, b: dot(mine(a), b), rows, w)
    back_own = order.step(lambda a, b: back(mine(a), b), cot, v)
    back_away = swapped(order.step(lambda a, b: back(others(a), b), cot, v_far), "tensor")
    gates = [v_far, arrived[0], arrived[0]]
    send(1)
    send(2)
    back_far = order.step(lambda a, b: back(mine(a), b), cot, v_far)
    v_all = order.step(
        lambda a, b: jnp.concatenate([jnp.where(j == 0, a, b), jnp.where(j == 0, b, a)], axis=0), v, v_far
    )
    summed, kept, returned, stream, normed, grads, near, across = {}, {}, {}, {}, {}, {}, {}, {}
    gain_part = None

    def multiply(c):
        half_of = lambda x, i: lax.dynamic_index_in_dim(x, i, 0, keepdims=False)
        summed[c] = swapped(order.step(lambda x: dot(half_of(x, 1 - k), w), arrived[c]), "tensor")
        gates.append(arrived[c])
        if c + 3 < count:
            send(c + 3)
        kept[c] = order.step(lambda x: dot(half_of(x, k), w), arrived[c])

    def give_back(c):
        returned[c] = swapped(order.step(lambda a, b: add(a, b).astype(bf16), kept[c], summed[c]), "dp")

    def finish_stream(c):
        t = takes[c]

        def fn(back_half, own, far, res):
            total = halves(add(own[t], far[t]), back_half.astype(f32))
            return (res[t].astype(f32) + scale * total).astype(bf16)

        stream[c] = shifted(order.step(fn, returned[c], mixed_own, mixed_near, resid), "pipe", 1)

    def normalise(c):
        nonlocal gain_part
        t = takes[c]

        def norm(s):
            s = s.astype(f32)
            inv = lax.rsqrt(jnp.mean(s * s, axis=-1, keepdims=True) + 1e-05)
            return ((s * inv) * gain_row).astype(bf16), inv

        normed[c], inv = order.step(norm, stream[c])
        got[c] = swapped(normed[c], "tensor")

        def finish(s, inv, own, own_in, far, cots):
            unit = s.astype(f32) * inv
            grad = halves(add(own[t], own_in[t]), far[t])
            gains = jnp.sum(grad * unit, axis=0)
            weighted = gain_row * grad
            centre = jnp.mean(weighted * unit, axis=-1, keepdims=True)
            return (cots[t].astype(f32) + inv * (weighted - unit * centre)).astype(bf16), gains

        out, gains = order.step(finish, stream[c], inv, back_own, back_near, grad_far, cot_stream)
        gain_part = gains if gain_part is None else gain_part + gains
        grads[c] = shifted(out, "pipe", -1)

    def project(c):
        near[c] = order.step(dot, normed[c], v_all)
        across[c] = order.step(dot, got[c], v_all)

    for i in range(count + 3):
        if i < count:
            multiply(i)
        if i == 1:
            grad_far = order.step(add, back_far, back_away)
        if 3 <= i:
            project(i - 3)
        if 2 <= i <= count + 1:
            normalise(i - 2)
        if i < count:
            give_back(i)
        if 1 <= i <= count:
            finish_stream(i - 1)
    beside = swapped(gain_part, "tensor")
    across_y = swapped(gain_part, "dp")
    opposite = lax.ppermute(gain_part, ("dp", "tensor"), [(i, 3 - i) for i in range(4)])
    gain_part = (gain_part + beside) + (across_y + opposite)

    def joined(parts):
        return jnp.concatenate([parts[c] for c in range(count)], 0)

    low, high = joined(near), joined(across)
    projected = jnp.concatenate([jnp.where(k == 0, low, high), jnp.where(k == 0, high, low)], 0)
    return joined(stream)[None, None], projected[None, None], joined(grads)[None, None], gain_part[None]


def solution(mesh):
    in_specs = (
        P("pipe", "dp", None, "tensor"),
        P("pipe", "tensor", "dp"),
        P("pipe", "dp", "tensor"),
        P("pipe", None),
        P("pipe", "dp", "tensor", None),
        P("pipe", "dp", None, "tensor"),
        P("pipe", "dp", "tensor", None),
    )
    out_specs = (
        P("pipe", "dp", "tensor", None),
        P("pipe", "dp", None, "tensor"),
        P("pipe", "dp", "tensor", None),
        P("pipe", None),
    )
    paired = mesh.shape["dp"] == 2 and mesh.shape["tensor"] == 2
    body = functools.partial(paired_body, SHARES) if paired else general_body
    return jax.shard_map(body, mesh=mesh, in_specs=in_specs, out_specs=out_specs, check_vma=False)
```
